32 devices in a mesh: groups: 2 (over y), strip: 4 (over z), visit: 2 (over x), band: 2 (over core).
Axes of the slice: x: 2, y: 2, z: 4, core: 2. Of those that a mesh axis runs over, the one named last changes fastest.
Arguments:
- observed: float32 [256, 128, 512], P(('groups', 'strip', 'visit')), parts along dimension 0, may hold values from -6 to 6
- home_strip: int32 [256, 1], P(('groups', 'strip', 'visit')), parts along dimension 0, may hold values from 0 to 3; in each aligned block of 16 rows (0 to 15, 16 to 31, ...) at most 8 rows name the same one
- column_block: int32 [256], P(('groups', 'strip', 'visit')), parts along dimension 0, may hold values from 0 to 28
- psf_index: int32 [256, 4], P(('groups', 'strip', 'visit')), parts along dimension 0, may hold values from 0 to 7
- psf_coeff: float32 [256, 4, 2], P(('groups', 'strip', 'visit')), parts along dimension 0, may hold values from 0.1 to 0.3
- weight: float32 [256], P(('groups', 'strip', 'visit')), parts along dimension 0, may hold values from 0.5 to 2
- kernels: float32 [8, 2, 17], replicated, may hold values from 0.01764706 to 0.052941177
- sky_model: float32 [1024, 4096], P(('groups', 'strip')), parts along dimension 0, may hold values from 0 to 1.5
Outputs:
- restored: float32 [1024, 4096], P(('groups', 'strip')), parts along dimension 0
The draws below stay inside these ranges and needn't reach their ends.
There are 2 independent parts, one for each index of `groups`. The reference program is written for one: setup_inputs(seed, part) draws one part's arguments, and reference() takes and returns one part's arrays. A program takes and returns all parts, laid end to end along the dimension named above; an argument that names none is the same for every part. Nothing has to cross between parts.
Inputs may be any that keep to these rules, and one draw needn't show every extreme that they name: `home_strip`: among the 16 tiles of one owner device (aligned blocks of 16 tiles), no strip is named more than 8 times; some strip is named exactly 8 times.
All inputs are finite; a program needn't handle non-finite values.
Results may differ from the reference program's by a relative error of at most 0.00014.
Values sent between devices are 32-bit elements; how exact they have to be, the bound alone decides.
A program may use at most 128 MiB of HBM per device.

```python
import math
import jax
import jax.numpy as jnp
import numpy as np
from jax import lax

PW = 4096
SROWS = 128
TW = 512
BLK = 128
R = 8
K = 4
NB = 8
STEPS = 1
TPD = 16
NT = 128
NROWS = 512
N_STRIP = 4
N_VISIT = 2


def plant(values, rng, least, top_value):
    shape = values.shape
    place = [jax.random.randint(jax.random.fold_in(rng, axis), (), 0, shape[axis]) for axis in range(len(shape))]
    values = values.at[tuple(place)].set(least)
    longest = shape.index(max(shape))
    place[longest] = (place[longest] + 1) % shape[longest]
    return values.at[tuple(place)].set(top_value)


def shard_levels(stream_key, shape, pieces, smallest, top_value):
    def one(dim, parts):
        heights = jax.random.uniform(jax.random.fold_in(jax.random.fold_in(stream_key, 6), dim), (parts,), jnp.float32, smallest / len(pieces), top_value / len(pieces))
        return jnp.repeat(jnp.exp(heights), shape[dim] // parts).reshape((-1,) + (1,) * (len(shape) - dim - 1))

    level = one(*pieces[0])
    for cut in pieces[1:]:
        level = level * one(*cut)
    return level


def assign_block(key, own, number, rows, count, top, most, skew):
    order = jax.random.permutation(key, count)
    crowded, ordinary = load_shares(count, rows * top, most, skew, True), load_shares(count, rows * top, most, skew, False)
    places = jnp.arange(count)

    def named(sizes, rotation):
        used = int((sizes > 0).sum())
        fixed = max(1, used // 4)
        passed = fixed + (places - fixed + rotation * (used - fixed)) % max(1, count - fixed)
        return jnp.zeros((count,), jnp.int32).at[order[jnp.where(places < fixed, places, passed)]].set(jnp.asarray(sizes, jnp.int32))

    sizes = jnp.where(number % 4 == 0, named(crowded, number // 4), named(ordinary, number - number // 4 - 1))
    mixed = jax.random.permutation(jax.random.fold_in(own, 3), count)
    source_of, taker = mixed[0:count // 2 * 2:2], mixed[1:count // 2 * 2:2]
    slack = jnp.minimum(sizes[source_of] - 1, most - sizes[taker]) // 2
    slack = jnp.where((source_of == order[0]) | (taker == order[0]) | (sizes[taker] == 0), 0, jnp.maximum(slack, 0))
    passed = jax.random.randint(jax.random.fold_in(own, 4), (count // 2,), 0, 1 << 20) % (slack + 1)
    sizes = sizes.at[source_of].add(-passed).at[taker].add(passed)
    members = jnp.searchsorted(jnp.cumsum(sizes), jnp.arange(rows * top), side="right").astype(jnp.int32)
    grid = members.reshape(top, rows).T
    grid = grid[jax.random.permutation(jax.random.fold_in(own, 1), rows)]
    rotation = jax.random.randint(jax.random.fold_in(own, 2), (rows, 1), 0, top)
    return jnp.take_along_axis(grid, (jnp.arange(top)[None, :] + rotation) % top, axis=1)


def load_shares(number_of, total, reach, lean, full):
    loads = [(1 << 20) // math.isqrt(standing ** lean) + 1 for standing in range(1, number_of + 1)]
    largest = reach if full else min(reach, max(-(-total // number_of), total * loads[0] // sum(loads)))
    least = 1 if total - largest >= number_of - 1 else 0
    given, surplus = [largest] + [least] * (number_of - 1), total - largest - least * (number_of - 1)
    while surplus > 0:
        free = [i for i in range(1, number_of) if given[i] < largest] or [i for i in range(1, number_of) if given[i] < reach]
        mass, left = sum([loads[i] for i in free]), surplus
        for i in free:
            more = min(reach - given[i], max(1, left * loads[i] // mass), surplus)
            given[i] = given[i] + more
            surplus = surplus - more
    return np.array(given)


def centred(own_key, shape, width, limit, split=(), kind=jnp.bfloat16):
    values = width * jax.random.normal(own_key, shape, jnp.float32)
    if split:
        values = values * shard_levels(own_key, shape, split, -0.22, 0.18)
    return jnp.clip(values, -limit, limit).astype(kind)


def setup_inputs(seed: int = 0, part: int = 0) -> dict:
    keys = jax.random.split(jax.random.key(seed), 9)
    part_keys = jax.random.split(jax.random.fold_in(keys[8], part), 9)
    observed = centred(part_keys[0], (NT, SROWS, TW), 1.0, 6.0, ((0, 8),), jnp.float32)
    home_strip_keys = jax.random.split(jax.random.fold_in(part_keys[1], 1), NT // TPD)
    home_strip_turns = jax.random.permutation(jax.random.fold_in(part_keys[1], 3), NT // TPD)
    home_strip = jax.vmap(lambda own, number: assign_block(jax.random.fold_in(part_keys[1], 2), own, number, TPD, N_STRIP, 1, 2 * TPD // N_STRIP, 2))(home_strip_keys, home_strip_turns).reshape((NT, 1))
    column_block = plant(jax.random.randint(part_keys[2], (NT,), 0, 4 * (PW - TW) // TW + 1), jax.random.fold_in(part_keys[2], 1), 0, (4 * (PW - TW) // TW + 1) - 1).astype(jnp.int32)
    psf_index = plant(jax.random.randint(part_keys[3], (NT, K), 0, NB), jax.random.fold_in(part_keys[3], 1), 0, NB - 1).astype(jnp.int32)
    psf_coeff = jnp.clip(0.1 + 0.20000001043081284 * jax.random.uniform(part_keys[4], (NT, K, 2), jnp.float32) ** shard_levels(part_keys[4], (NT, K, 2), ((0, 8),), -0.2, 0.2), 0.1, 0.3)
    weight = jnp.clip(jnp.exp(math.log(2.0) - 1.3862944 * jax.random.uniform(part_keys[5], (NT,), jnp.float32) ** shard_levels(part_keys[5], (NT,), ((0, 8),), -0.2, 0.2)), 0.5, 2.0)
    kernels = jnp.clip(jax.random.uniform(keys[6], (NB, 2, 2 * R + 1), jnp.float32, 0.01764706, 0.052941177), 0.01764706, 0.052941177)
    sky_model = jnp.clip(1.5 * jax.random.uniform(part_keys[7], (NROWS, PW), jnp.float32) ** shard_levels(part_keys[7], (NROWS, PW), ((0, 4),), -0.2, 0.2), 0.0, 1.5)
    return {"observed": observed, "home_strip": home_strip, "column_block": column_block, "psf_index": psf_index, "psf_coeff": psf_coeff, "weight": weight, "kernels": kernels, "sky_model": sky_model}


highest = lax.Precision.HIGHEST
step_size = 0.5


def band_matrix(kernel_taps, height, breadth):
    distance = jnp.arange(breadth)[None, :] - jnp.arange(height)[:, None]
    inside = (distance >= 0) & (distance < kernel_taps.shape[0])
    picked = kernel_taps[jnp.clip(distance, 0, kernel_taps.shape[0] - 1)]
    return jnp.where(inside, picked, jnp.zeros_like(picked))


def build_banks(kernels):
    row_matrices = jax.vmap(lambda k: band_matrix(k, SROWS, SROWS + 2 * R))(kernels[:, 0])
    column_matrices = jax.vmap(lambda k: band_matrix(k, BLK, BLK + 2 * R))(kernels[:, 1])
    return row_matrices, column_matrices


def psf_scales(psf_coeff):
    across = (jnp.arange(TW).astype(psf_coeff.dtype) + 0.5) / TW - 0.5
    return psf_coeff[..., 0:1] + psf_coeff[..., 1:2] * across


def forward(windows, row_pick, column_pick, psf_scale):
    row_conv = jnp.einsum('skij,sjc->skic', row_pick, windows, precision=highest)
    block_width = column_pick.shape[-2]
    block_reach = column_pick.shape[-1]
    block_count = psf_scale.shape[-1] // block_width
    blocks = jnp.stack([row_conv[..., q * block_width:q * block_width + block_reach] for q in range(block_count)], axis=2)
    convolved = jnp.einsum('skqic,skbc->skiqb', blocks, column_pick, precision=highest)
    convolved = convolved.reshape(row_conv.shape[0], row_conv.shape[1], row_conv.shape[2], psf_scale.shape[-1])
    return jnp.sum(psf_scale[:, :, None, :] * convolved, 1)


def adjoint(weighted, row_pick, column_pick, psf_scale):
    spread = psf_scale[:, :, None, :] * weighted[:, None]
    block_width = column_pick.shape[-2]
    block_reach = column_pick.shape[-1]
    total_cols = spread.shape[-1]
    block_count = total_cols // block_width
    shaped = spread.reshape(spread.shape[0], spread.shape[1], spread.shape[2], block_count, block_width)
    back_cols = jnp.einsum('skiqb,skbc->skqic', shaped, column_pick, precision=highest)
    extent = total_cols + block_reach - block_width
    summed = jnp.zeros(back_cols.shape[:2] + (back_cols.shape[3], extent), back_cols.dtype)
    for q in range(block_count):
        before = q * block_width
        summed = summed + jnp.pad(back_cols[:, :, q], ((0, 0), (0, 0), (0, 0), (before, extent - before - block_reach)))
    return jnp.einsum('skij,skic->sjc', row_pick, summed, precision=highest)


def reference(observed, home_strip, column_block, psf_index, psf_coeff, weight, kernels, sky_model):
    row_matrices, column_matrices = build_banks(kernels)
    owners = N_STRIP * N_VISIT

    def shaped(array):
        return array.reshape((owners, TPD) + array.shape[1:])

    starts = (column_block * (TW // 4)).astype(jnp.int32)
    tops = (home_strip[:, 0] * SROWS).astype(jnp.int32)
    for iteration in range(STEPS):
        padded = jnp.pad(sky_model, ((R, R), (R, R)))

        def visit_block(accum, block):
            seen, tops_here, starts_here, index_here, coeff_here, weight_here = block
            windows = jax.vmap(lambda t, s: lax.dynamic_slice(padded, (t, s), (SROWS + 2 * R, TW + 2 * R)))(tops_here, starts_here)
            row_pick = row_matrices[index_here]
            column_pick = column_matrices[index_here]
            psf_scale = psf_scales(coeff_here)
            predicted = forward(windows, row_pick, column_pick, psf_scale)
            weighted = weight_here[:, None, None] * (predicted - seen)
            tile_grads = adjoint(weighted, row_pick, column_pick, psf_scale)

            def accumulate(i, grad_sum):
                current = lax.dynamic_slice(grad_sum, (tops_here[i], starts_here[i]), tile_grads.shape[1:])
                return lax.dynamic_update_slice(grad_sum, current + tile_grads[i], (tops_here[i], starts_here[i]))

            return lax.fori_loop(0, TPD, accumulate, accum), None

        grad_sum, unused = lax.scan(visit_block, jnp.zeros_like(padded), (shaped(observed), shaped(tops), shaped(starts), shaped(psf_index), shaped(psf_coeff), shaped(weight)))
        gradient = grad_sum[R:R + NROWS, R:R + PW]
        sky_model = jnp.maximum(sky_model - step_size * gradient, 0.0)
    return sky_model
```

```python
import functools

import jax
import jax.numpy as jnp
from jax import lax
from jax.experimental import pallas as pl
from jax.experimental.pallas import tpu as pltpu
from jax.sharding import PartitionSpec as P

PW = 4096
SROWS = 128
TW = 512
R = 8
K = 4
TPD = 16
LANE = 128
REACH = SROWS + 2 * R
MW = PW + 2 * LANE
VIEW = TW + 2 * LANE
EXT = TW + LANE
QROWS = K * LANE + LANE
f32, bf16 = jnp.float32, jnp.bfloat16
step_size = 0.5


def split(x):
    hi = x.astype(bf16)
    return hi, (x - hi.astype(f32)).astype(bf16)


def split_outside(x):
    hi = lax.reduce_precision(x, 8, 7)
    return hi.astype(bf16), (x - hi).astype(bf16)


def banded(taps, height, breadth, offset_of):
    rows = lax.broadcasted_iota(jnp.int32, (1, height, breadth), 1)
    cols = lax.broadcasted_iota(jnp.int32, (1, height, breadth), 2)
    distance = offset_of(rows, cols)
    total = jnp.zeros((taps.shape[0], height, breadth), f32)
    for d in range(taps.shape[1]):
        total = total + jnp.where(distance == d, taps[:, d][:, None, None], 0.0)
    return total


def banks(kernels):
    row = banded(kernels[:, 0], SROWS, REACH, lambda i, j: j - i)
    rowt = banded(kernels[:, 0], REACH, SROWS, lambda j, i: j - i)
    colt = banded(kernels[:, 1], REACH, LANE, lambda c, b: c - b)
    hi, lo = split_outside(row)
    prow = jnp.concatenate([hi, lo, hi], 2)
    prow = jnp.pad(prow, ((0, 0), (0, 0), (0, 512 - 3 * REACH)))
    thi, tlo = split_outside(rowt)
    return prow, thi, tlo, colt


def mm(a, b):
    return lax.dot_general(a, b, (((1,), (0,)), ((), ())), preferred_element_type=f32)


def mmt(a, b):
    return lax.dot_general(a, b, (((1,), (1,)), ((), ())), preferred_element_type=f32)


def tiles_kernel(
    home, block, index, coeff, weight, sky, obs, prow, thi, tlo, colt,
    acc, wcat, pcat, lhi, llo, qhi, qlo, bhi, blo, pthi, ptlo, views, seen, sems,
):
    acc[...] = jnp.zeros_like(acc)
    wcat[...] = jnp.zeros_like(wcat)
    qhi[...] = jnp.zeros_like(qhi)
    qlo[...] = jnp.zeros_like(qlo)
    band = lax.axis_index("band")
    count = TPD // lax.axis_size("band")
    lane = lax.broadcasted_iota(jnp.int32, (SROWS, LANE), 1)
    tail = lane < 2 * R
    across = (lane.astype(f32) + 0.5) / TW - 0.5

    def fetches(i):
        t, slot = band * count + i, i % 2
        top = pl.multiple_of(home[t, 0] * SROWS, SROWS)
        start = pl.multiple_of(block[t] * LANE, LANE)
        return (
            pltpu.make_async_copy(
                sky.at[pl.ds(top, REACH), pl.ds(start, VIEW)], views.at[slot], sems.at[0, slot]
            ),
            pltpu.make_async_copy(obs.at[t], seen.at[slot], sems.at[1, slot]),
        )

    for copy in fetches(0):
        copy.start()

    def one(i, carry):
        t, slot = band * count + i, i % 2

        @pl.when(i + 1 < count)
        def _():
            for copy in fetches(i + 1):
                copy.start()

        for copy in fetches(i):
            copy.wait()
        top = pl.multiple_of(home[t, 0] * SROWS, SROWS)
        start = pl.multiple_of(block[t] * LANE, LANE)
        window = pltpu.roll(views[slot], VIEW - (LANE - R), 1)[:, :EXT]
        whi, wlo = split(window)
        wcat[0:REACH, :] = whi
        wcat[REACH : 2 * REACH, :] = whi
        wcat[2 * REACH : 3 * REACH, :] = wlo
        for k in range(K):
            n = index[t, k]
            pcat[k * SROWS : (k + 1) * SROWS, :] = prow[n]
            pthi[:, k * SROWS : (k + 1) * SROWS] = thi[n]
            ptlo[:, k * SROWS : (k + 1) * SROWS] = tlo[n]
            taps = colt[n]
            for half in range(2):
                hi, lo = split(taps * coeff[t, 2 * k + half])
                side = slice(half * LANE, (half + 1) * LANE)
                qhi[k * LANE : (k + 1) * LANE, side] = hi[:LANE]
                qlo[k * LANE : (k + 1) * LANE, side] = lo[:LANE]
                at = K * LANE + 2 * R * k
                qhi[at : at + 2 * R, side] = hi[LANE:]
                qlo[at : at + 2 * R, side] = lo[LANE:]
        rowed = mm(pcat[...], wcat[...])
        for q in range(TW // LANE):
            rows = slice(q * LANE, (q + 1) * LANE)
            packed = jnp.zeros((SROWS, LANE), f32)
            for k in range(K):
                part = rowed[k * SROWS : (k + 1) * SROWS]
                hi, lo = split(part[:, q * LANE : (q + 1) * LANE])
                lhi[rows, k * LANE : (k + 1) * LANE] = hi
                llo[rows, k * LANE : (k + 1) * LANE] = lo
                end = jnp.where(tail, part[:, (q + 1) * LANE : (q + 2) * LANE], 0.0)
                packed = packed + (pltpu.roll(end, 2 * R * k, 1) if k else end)
            hi, lo = split(packed)
            lhi[rows, K * LANE :] = hi
            llo[rows, K * LANE :] = lo
        both = mm(lhi[...], qhi[...]) + mm(lhi[...], qlo[...]) + mm(llo[...], qhi[...])
        factor = weight[t]
        spread = []
        for q in range(TW // LANE):
            rows = slice(q * LANE, (q + 1) * LANE)
            at = across + q * LANE / TW
            predicted = both[rows, :LANE] + at * both[rows, LANE:]
            weighted = factor * (predicted - seen[slot, :, q * LANE : (q + 1) * LANE])
            spread.append(jnp.concatenate([weighted, at * weighted], 1))
        shi, slo = split(jnp.concatenate(spread, 0))
        back = mmt(shi, qhi[...]) + mmt(shi, qlo[...]) + mmt(slo, qhi[...])
        for m in range(TW // LANE + 1):
            for k in range(K):
                total = 0.0
                if m < TW // LANE:
                    total = back[m * LANE : (m + 1) * LANE, k * LANE : (k + 1) * LANE]
                if m > 0:
                    end = back[(m - 1) * LANE : m * LANE, K * LANE :]
                    end = pltpu.roll(end, LANE - 2 * R * k, 1) if k else end
                    total = total + jnp.where(tail, end, 0.0)
                hi, lo = split(total)
                bhi[k * SROWS : (k + 1) * SROWS, m * LANE : (m + 1) * LANE] = hi
                blo[k * SROWS : (k + 1) * SROWS, m * LANE : (m + 1) * LANE] = lo
        grad = mm(pthi[...], bhi[...]) + mm(pthi[...], blo[...]) + mm(ptlo[...], bhi[...])
        grad = jnp.concatenate([grad, jnp.zeros((REACH, LANE), f32)], 1)
        grad = pltpu.roll(grad, LANE - R, 1)
        here = (pl.ds(top, REACH), pl.ds(start, VIEW))
        acc[here] = acc[here] + grad
        return carry

    lax.fori_loop(0, count, one, 0)


def tile_gradients(home, block, index, coeff, weight, sky, obs, bank):
    vmem = pl.BlockSpec(memory_space=pltpu.VMEM)
    smem = pl.BlockSpec(memory_space=pltpu.SMEM)
    return pl.pallas_call(
        tiles_kernel,
        out_shape=jax.ShapeDtypeStruct(sky.shape, f32),
        in_specs=[smem] * 5 + [pl.BlockSpec(memory_space=pl.ANY)] * 2 + [vmem] * 4,
        out_specs=vmem,
        scratch_shapes=[
            pltpu.VMEM((512, EXT), bf16),
            pltpu.VMEM((K * SROWS, 512), bf16),
            pltpu.VMEM((TW, QROWS), bf16),
            pltpu.VMEM((TW, QROWS), bf16),
            pltpu.VMEM((QROWS, 2 * LANE), bf16),
            pltpu.VMEM((QROWS, 2 * LANE), bf16),
            pltpu.VMEM((K * SROWS, EXT), bf16),
            pltpu.VMEM((K * SROWS, EXT), bf16),
            pltpu.VMEM((REACH, K * SROWS), bf16),
            pltpu.VMEM((REACH, K * SROWS), bf16),
            pltpu.VMEM((2, REACH, VIEW), f32),
            pltpu.VMEM((2, SROWS, TW), f32),
            pltpu.SemaphoreType.DMA((2, 2)),
        ],
        compiler_params=pltpu.CompilerParams(vmem_limit_bytes=56 * 2**20),
    )(home, block, index, coeff.reshape(TPD, 2 * K), weight, sky, obs, *bank)


def on_device(observed, home_strip, column_block, psf_index, psf_coeff, weight, kernels, sky_model):
    visits, bands = lax.axis_size("visit"), lax.axis_size("band")
    piece = PW // (visits * bands)
    at = (lax.axis_index("visit") * bands + lax.axis_index("band")) * piece
    mine = lax.dynamic_slice_in_dim(sky_model, at, piece, 1)
    whole = lax.all_gather(mine, "strip", axis=0, tiled=True)
    whole = lax.all_gather(whole, "visit", axis=0)
    whole = lax.all_gather(whole, "band", axis=1)
    sky = jnp.zeros((whole.shape[2] + 2 * R, MW), f32)
    for v in range(visits):
        for b in range(bands):
            sky = lax.dynamic_update_slice(sky, whole[v, b], (R, LANE + (v * bands + b) * piece))
    bank = banks(kernels)
    grads = tile_gradients(
        home_strip, column_block, psf_index, psf_coeff, weight, sky, observed, bank
    )
    grads = grads[R:-R, LANE:-LANE].reshape(-1, visits, bands, piece).transpose(2, 1, 0, 3)
    grads = lax.psum_scatter(grads, "band", scatter_dimension=0)
    grads = lax.psum_scatter(grads, "visit", scatter_dimension=0)
    grads = lax.psum_scatter(grads, "strip", scatter_dimension=0, tiled=True)
    new = jnp.maximum(mine - step_size * grads, 0.0)
    new = lax.all_gather(new, ("visit", "band"), axis=1, tiled=True)
    return new


def solution(mesh):
    tiles = ("groups", "strip", "visit")
    placed = (
        P(tiles, None, None),
        P(tiles, None),
        P(tiles),
        P(tiles, None),
        P(tiles, None, None),
        P(tiles),
        P(),
        P(("groups", "strip"), None),
    )
    return jax.shard_map(
        on_device,
        mesh=mesh,
        in_specs=placed,
        out_specs=P(("groups", "strip"), None),
        check_vma=False,
    )
```

```python
import functools

import jax
import jax.numpy as jnp
from jax import lax
from jax.experimental import pallas as pl
from jax.experimental.pallas import tpu as pltpu
from jax.sharding import PartitionSpec as P

PW = 4096
SROWS = 128
TW = 512
R = 8
K = 4
TPD = 16
LANE = 128
REACH = SROWS + 2 * R
MW = PW + 2 * LANE
VIEW = TW + 2 * LANE
EXT = TW + LANE
QROWS = K * LANE + LANE
f32, bf16 = jnp.float32, jnp.bfloat16
step_size = 0.5


def split(x):
    hi = x.astype(bf16)
    return hi, (x - hi.astype(f32)).astype(bf16)


def split_outside(x):
    hi = lax.reduce_precision(x, 8, 7)
    return hi.astype(bf16), (x - hi).astype(bf16)


def banded(taps, height, breadth, offset_of):
    rows = lax.broadcasted_iota(jnp.int32, (1, height, breadth), 1)
    cols = lax.broadcasted_iota(jnp.int32, (1, height, breadth), 2)
    distance = offset_of(rows, cols)
    total = jnp.zeros((taps.shape[0], height, breadth), f32)
    for d in range(taps.shape[1]):
        total = total + jnp.where(distance == d, taps[:, d][:, None, None], 0.0)
    return total


def banks(kernels):
    row = banded(kernels[:, 0], SROWS, REACH, lambda i, j: j - i)
    rowt = banded(kernels[:, 0], REACH, SROWS, lambda j, i: j - i)
    colt = banded(kernels[:, 1], REACH, LANE, lambda c, b: c - b)
    hi, lo = split_outside(row)
    prow = jnp.concatenate([hi, lo, hi], 2)
    prow = jnp.pad(prow, ((0, 0), (0, 0), (0, 512 - 3 * REACH)))
    thi, tlo = split_outside(rowt)
    return prow, thi, tlo, colt


def mm(a, b):
    return lax.dot_general(a, b, (((1,), (0,)), ((), ())), preferred_element_type=f32)


def mmt(a, b):
    return lax.dot_general(a, b, (((1,), (1,)), ((), ())), preferred_element_type=f32)


def tiles_kernel(
    home, block, index, coeff, weight, sky, obs, prow, thi, tlo, colt,
    acc, wcat, pcat, lhi, llo, qhi, qlo, bhi, blo, pthi, ptlo, views, seen, sems,
):
    acc[...] = jnp.zeros_like(acc)
    wcat[...] = jnp.zeros_like(wcat)
    qhi[...] = jnp.zeros_like(qhi)
    qlo[...] = jnp.zeros_like(qlo)
    band = lax.axis_index("band")
    count = TPD // lax.axis_size("band")
    lane = lax.broadcasted_iota(jnp.int32, (SROWS, LANE), 1)
    tail = lane < 2 * R
    across = (lane.astype(f32) + 0.5) / TW - 0.5

    def fetches(i):
        t, slot = band * count + i, i % 2
        top = pl.multiple_of(home[t, 0] * SROWS, SROWS)
        start = pl.multiple_of(block[t] * LANE, LANE)
        return (
            pltpu.make_async_copy(
                sky.at[pl.ds(top, REACH), pl.ds(start, VIEW)], views.at[slot], sems.at[0, slot]
            ),
            pltpu.make_async_copy(obs.at[t], seen.at[slot], sems.at[1, slot]),
        )

    for copy in fetches(0):
        copy.start()

    def one(i, carry):
        t, slot = band * count + i, i % 2

        @pl.when(i + 1 < count)
        def _():
            for copy in fetches(i + 1):
                copy.start()

        for copy in fetches(i):
            copy.wait()
        top = pl.multiple_of(home[t, 0] * SROWS, SROWS)
        start = pl.multiple_of(block[t] * LANE, LANE)
        window = pltpu.roll(views[slot], VIEW - (LANE - R), 1)[:, :EXT]
        whi, wlo = split(window)
        wcat[0:REACH, :] = whi
        wcat[REACH : 2 * REACH, :] = whi
        wcat[2 * REACH : 3 * REACH, :] = wlo
        for k in range(K):
            n = index[t, k]
            pcat[k * SROWS : (k + 1) * SROWS, :] = prow[n]
            pthi[:, k * SROWS : (k + 1) * SROWS] = thi[n]
            ptlo[:, k * SROWS : (k + 1) * SROWS] = tlo[n]
            taps = colt[n]
            for half in range(2):
                hi, lo = split(taps * coeff[t, 2 * k + half])
                side = slice(half * LANE, (half + 1) * LANE)
                qhi[k * LANE : (k + 1) * LANE, side] = hi[:LANE]
                qlo[k * LANE : (k + 1) * LANE, side] = lo[:LANE]
                at = K * LANE + 2 * R * k
                qhi[at : at + 2 * R, side] = hi[LANE:]
                qlo[at : at + 2 * R, side] = lo[LANE:]
        rowed = mm(pcat[...], wcat[...])
        for q in range(TW // LANE):
            rows = slice(q * LANE, (q + 1) * LANE)
            packed = jnp.zeros((SROWS, LANE), f32)
            for k in range(K):
                part = rowed[k * SROWS : (k + 1) * SROWS]
                hi, lo = split(part[:, q * LANE : (q + 1) * LANE])
                lhi[rows, k * LANE : (k + 1) * LANE] = hi
                llo[rows, k * LANE : (k + 1) * LANE] = lo
                end = jnp.where(tail, part[:, (q + 1) * LANE : (q + 2) * LANE], 0.0)
                packed = packed + (pltpu.roll(end, 2 * R * k, 1) if k else end)
            hi, lo = split(packed)
            lhi[rows, K * LANE :] = hi
            llo[rows, K * LANE :] = lo
        both = mm(lhi[...], qhi[...]) + mm(lhi[...], qlo[...]) + mm(llo[...], qhi[...])
        factor = weight[t]
        spread = []
        for q in range(TW // LANE):
            rows = slice(q * LANE, (q + 1) * LANE)
            at = across + q * LANE / TW
            predicted = both[rows, :LANE] + at * both[rows, LANE:]
            weighted = factor * (predicted - seen[slot, :, q * LANE : (q + 1) * LANE])
            spread.append(jnp.concatenate([weighted, at * weighted], 1))
        shi, slo = split(jnp.concatenate(spread, 0))
        back = mmt(shi, qhi[...]) + mmt(shi, qlo[...]) + mmt(slo, qhi[...])
        for m in range(TW // LANE + 1):
            for k in range(K):
                total = 0.0
                if m < TW // LANE:
                    total = back[m * LANE : (m + 1) * LANE, k * LANE : (k + 1) * LANE]
                if m > 0:
                    end = back[(m - 1) * LANE : m * LANE, K * LANE :]
                    end = pltpu.roll(end, LANE - 2 * R * k, 1) if k else end
                    total = total + jnp.where(tail, end, 0.0)
                hi, lo = split(total)
                bhi[k * SROWS : (k + 1) * SROWS, m * LANE : (m + 1) * LANE] = hi
                blo[k * SROWS : (k + 1) * SROWS, m * LANE : (m + 1) * LANE] = lo
        grad = mm(pthi[...], bhi[...]) + mm(pthi[...], blo[...]) + mm(ptlo[...], bhi[...])
        grad = jnp.concatenate([grad, jnp.zeros((REACH, LANE), f32)], 1)
        grad = pltpu.roll(grad, LANE - R, 1)
        here = (pl.ds(top, REACH), pl.ds(start, VIEW))
        acc[here] = acc[here] + grad
        return carry

    lax.fori_loop(0, count, one, 0)


def tile_gradients(home, block, index, coeff, weight, sky, obs, bank):
    vmem = pl.BlockSpec(memory_space=pltpu.VMEM)
    smem = pl.BlockSpec(memory_space=pltpu.SMEM)
    return pl.pallas_call(
        tiles_kernel,
        out_shape=jax.ShapeDtypeStruct(sky.shape, f32),
        in_specs=[smem] * 5 + [pl.BlockSpec(memory_space=pl.ANY)] * 2 + [vmem] * 4,
        out_specs=vmem,
        scratch_shapes=[
            pltpu.VMEM((512, EXT), bf16),
            pltpu.VMEM((K * SROWS, 512), bf16),
            pltpu.VMEM((TW, QROWS), bf16),
            pltpu.VMEM((TW, QROWS), bf16),
            pltpu.VMEM((QROWS, 2 * LANE), bf16),
            pltpu.VMEM((QROWS, 2 * LANE), bf16),
            pltpu.VMEM((K * SROWS, EXT), bf16),
            pltpu.VMEM((K * SROWS, EXT), bf16),
            pltpu.VMEM((REACH, K * SROWS), bf16),
            pltpu.VMEM((REACH, K * SROWS), bf16),
            pltpu.VMEM((2, REACH, VIEW), f32),
            pltpu.VMEM((2, SROWS, TW), f32),
            pltpu.SemaphoreType.DMA((2, 2)),
        ],
        compiler_params=pltpu.CompilerParams(vmem_limit_bytes=56 * 2**20),
    )(home, block, index, coeff.reshape(TPD, 2 * K), weight, sky, obs, *bank)


MESH = pl.DeviceIdType.MESH
CHUNKS = 2


def greet(strips, visits, bands):
    me, v, b = (lax.axis_index(a) for a in ("strip", "visit", "band"))
    barrier = pltpu.get_barrier_semaphore()

    def signal(axis, other):
        pl.semaphore_signal(barrier, inc=1, device_id={axis: other}, device_id_type=MESH)

    @pl.when(me > 0)
    def _():
        signal("strip", me - 1)

    @pl.when(me < strips - 1)
    def _():
        signal("strip", me + 1)

    for e in range(1, visits):
        signal("visit", lax.rem(v + e, visits))
    for e in range(1, bands):
        signal("band", lax.rem(b + e, bands))

    peers = visits + bands - 2 + (me > 0).astype(jnp.int32) + (me < strips - 1).astype(jnp.int32)
    pl.semaphore_wait(barrier, peers)


def gather_kernel(
    strips, visits, bands, sky, out, edge, side,
    own_sem, edge_sem, side_sem, zs, zr, xs, xr, bs, br,
):
    me, v, b = (lax.axis_index(a) for a in ("strip", "visit", "band"))
    piece = PW // (visits * bands)
    height = SROWS // CHUNKS
    other = lax.rem(b + 1, bands)
    edge[...] = jnp.zeros_like(edge)
    side[...] = jnp.zeros_like(side)
    local = [
        pltpu.make_async_copy(
            sky,
            out.at[pl.ds(pl.multiple_of(R + me * SROWS, 8), SROWS), pl.ds(LANE, PW)],
            own_sem,
        ),
        pltpu.make_async_copy(edge, out.at[pl.ds(0, R)], edge_sem.at[0]),
        pltpu.make_async_copy(edge, out.at[pl.ds(R + strips * SROWS, R)], edge_sem.at[1]),
    ]
    for s in range(strips):
        rows = pl.ds(R + s * SROWS, SROWS)
        local.append(pltpu.make_async_copy(side, out.at[rows, pl.ds(0, LANE)], side_sem.at[0, s]))
        local.append(
            pltpu.make_async_copy(side, out.at[rows, pl.ds(LANE + PW, LANE)], side_sem.at[1, s])
        )
    greet(strips, visits, bands)

    def spot(s, c, h):
        return out.at[
            pl.ds(pl.multiple_of(R + s * SROWS + h * height, 8), height),
            pl.ds(pl.multiple_of(LANE + c * piece, LANE), piece),
        ]

    def remote(src, dst, send, recv, axis, target):
        return pltpu.make_async_remote_copy(
            src_ref=src, dst_ref=dst, send_sem=send, recv_sem=recv,
            device_id={axis: target}, device_id_type=MESH,
        )

    mine = v * bands + b

    def hop(way, d, h, incoming):
        sign = 1 if way == 0 else -1
        s = me - sign * (d if incoming else d - 1)
        dst = spot(s, mine, h)
        if d == 1 and not incoming:
            src = sky.at[
                pl.ds(h * height, height), pl.ds(pl.multiple_of(mine * piece, LANE), piece)
            ]
        else:
            src = dst
        return remote(src, dst, zs.at[way, d - 1, h], zr.at[way, d - 1, h], "strip", me + sign)

    def can_send(way, d):
        return (me < strips - 1) & (me >= d - 1) if way == 0 else (me > 0) & (me + d - 1 < strips)

    def can_get(way, d):
        return me >= d if way == 0 else me + d < strips

    def across(way, d, h, e, incoming):
        s = me - d if way == 0 else me + d
        owner = lax.rem(v - e + visits, visits) if incoming else v
        at = spot(s, owner * bands + b, h)
        return remote(
            at, at, xs.at[way, d - 1, h, e - 1], xr.at[way, d - 1, h, e - 1],
            "visit", lax.rem(v + e, visits),
        )

    def beside(way, d, h, e, incoming):
        s = me - d if way == 0 else me + d
        at = spot(s, lax.rem(v - e + visits, visits) * bands + (other if incoming else b), h)
        return remote(at, at, bs.at[way, d - 1, h, e], br.at[way, d - 1, h, e], "band", other)

    for h in range(CHUNKS):
        for way in range(2):

            @pl.when(can_send(way, 1))
            def _():
                hop(way, 1, h, False).start()

    for copy in local:
        copy.start()
    for d in range(1, strips):
        for h in range(CHUNKS):
            for way in range(2):

                @pl.when(can_get(way, d))
                def _():
                    hop(way, d, h, True).wait_recv()
                    if d + 1 < strips:

                        @pl.when(can_send(way, d + 1))
                        def _():
                            hop(way, d + 1, h, False).start()

                    for e in range(1, visits):
                        across(way, d, h, e, False).start()
                    beside(way, d, h, 0, False).start()

        for h in range(CHUNKS):
            for way in range(2):
                if d < 2:
                    continue

                @pl.when(can_get(way, d - 1))
                def _():
                    for e in range(1, visits):
                        across(way, d - 1, h, e, True).wait_recv()
                        beside(way, d - 1, h, e, False).start()

    for h in range(CHUNKS):
        for way in range(2):

            @pl.when(can_get(way, strips - 1))
            def _():
                for e in range(1, visits):
                    across(way, strips - 1, h, e, True).wait_recv()
                    beside(way, strips - 1, h, e, False).start()

    for d in range(1, strips):
        for h in range(CHUNKS):
            for way in range(2):

                @pl.when(can_send(way, d))
                def _():
                    hop(way, d, h, False).wait_send()

                @pl.when(can_get(way, d))
                def _():
                    for e in range(1, visits):
                        across(way, d, h, e, False).wait_send()
                    for e in range(visits):
                        beside(way, d, h, e, False).wait_send()
                        beside(way, d, h, e, True).wait_recv()

    for copy in local:
        copy.wait()


def gather_sky(sky, strips, visits, bands):
    dma = pltpu.SemaphoreType.DMA
    hbm = pl.BlockSpec(memory_space=pl.ANY)
    steps = strips - 1
    return pl.pallas_call(
        functools.partial(gather_kernel, strips, visits, bands),
        out_shape=jax.ShapeDtypeStruct((strips * SROWS + 2 * R, MW), f32),
        in_specs=[hbm],
        out_specs=hbm,
        scratch_shapes=[
            pltpu.VMEM((R, MW), f32),
            pltpu.VMEM((SROWS, LANE), f32),
            dma,
            dma((2,)),
            dma((2, strips)),
            dma((2, steps, CHUNKS)),
            dma((2, steps, CHUNKS)),
            dma((2, steps, CHUNKS, visits - 1)),
            dma((2, steps, CHUNKS, visits - 1)),
            dma((2, steps, CHUNKS, visits)),
            dma((2, steps, CHUNKS, visits)),
        ],
        compiler_params=pltpu.CompilerParams(collective_id=0, has_side_effects=True),
    )(sky)


def reduce_kernel(
    strips, visits, bands, grad, sky, out, loc, bbuf, xbuf, zbuf, mine, new,
    loc_sem, mine_sem, new_sem, bs, br, xs, xr, zs, zr, ns, nr, ps, pr,
):
    me, v, b = (lax.axis_index(a) for a in ("strip", "visit", "band"))
    piece = PW // (visits * bands)
    other = lax.rem(b + 1, bands)

    def columns(c, margin):
        return pl.ds(pl.multiple_of(margin + c * piece, LANE), piece)

    def spot(s, c):
        return grad.at[pl.ds(pl.multiple_of(R + s * SROWS, 8), SROWS), columns(c, LANE)]

    def remote(src, dst, send, recv, axis, target):
        return pltpu.make_async_remote_copy(
            src_ref=src, dst_ref=dst, send_sem=send, recv_sem=recv,
            device_id={axis: target}, device_id_type=MESH,
        )

    order = [(way, d) for d in range(strips - 1, 0, -1) for way in range(2)] + [(0, 0)]

    def strip_of(way, d):
        return me + d if way == 0 else me - d

    def there(way, d):
        return me + d < strips if way == 0 else me >= d

    def visit_at(e):
        return lax.rem(v + e, visits)

    def load(j, s, e):
        return pltpu.make_async_copy(
            spot(s, visit_at(e) * bands + b), loc.at[s, e], loc_sem.at[j, e]
        )

    def beside(j, s, e):
        return remote(
            spot(s, visit_at(e) * bands + other), bbuf.at[s, e],
            bs.at[j, e], br.at[j, e], "band", other,
        )

    def across(j, s, e):
        return remote(
            loc.at[s, e], xbuf.at[s, e - 1], xs.at[j, e - 1], xr.at[j, e - 1],
            "visit", visit_at(e),
        )

    def hop(way, d):
        sign = 1 if way == 0 else -1
        s = strip_of(way, d)
        return remote(
            loc.at[s, 0], zbuf.at[way, s], zs.at[way, d - 1], zr.at[way, d - 1],
            "strip", me + sign,
        )

    def came(way, d):
        sign = 1 if way == 0 else -1
        s = strip_of(way, d)
        return remote(
            loc.at[s, 0], zbuf.at[way, s], zs.at[way, d], zr.at[way, d], "strip", me - sign
        )

    def behind(way):
        return me > 0 if way == 0 else me < strips - 1

    keep = pltpu.make_async_copy(sky.at[:, columns(v * bands + b, 0)], mine, mine_sem)
    greet(strips, visits, bands)
    for j, (way, d) in enumerate(order):

        @pl.when(there(way, d))
        def _():
            s = strip_of(way, d)
            for e in [*range(1, visits), 0]:
                beside(j, s, e).start()
                load(j, s, e).start()

    keep.start()

    def first(j, way, d):
        s = strip_of(way, d)
        for e in [*range(1, visits), 0]:
            load(j, s, e).wait()
            beside(j, s, e).wait_recv()
            loc[s, e] = loc[s, e] + bbuf[s, e]
            if e:
                across(j, s, e).start()

    def second(j, way, d):
        s = strip_of(way, d)
        for e in range(1, visits):
            across(j, s, e).wait_recv()
            loc[s, 0] = loc[s, 0] + xbuf[s, e - 1]
        if d:

            @pl.when(behind(way))
            def _():
                came(way, d).wait_recv()
                loc[s, 0] = loc[s, 0] + zbuf[way, s]

            hop(way, d).start()

    for j, (way, d) in enumerate(order):

        @pl.when(there(way, d))
        def _():
            first(j, way, d)

    for j, (way, d) in enumerate(order):

        @pl.when(there(way, d))
        def _():
            second(j, way, d)

    for way in range(2):

        @pl.when(behind(way))
        def _():
            came(way, 0).wait_recv()
            loc[me, 0] = loc[me, 0] + zbuf[way, me]

    keep.wait()
    new[...] = jnp.maximum(mine[...] - step_size * loc[me, 0], 0.0)

    def place(c):
        return out.at[:, columns(c, 0)]

    own = v * bands + b
    write = pltpu.make_async_copy(new, place(own), new_sem)

    def spread(e, incoming):
        c = lax.rem(v - e + visits, visits) * bands + b if incoming else own
        return remote(new, place(c), ns.at[e - 1], nr.at[e - 1], "visit", visit_at(e))

    def passed(e, incoming):
        c = lax.rem(v - e + visits, visits) * bands
        dst = place(c + (other if incoming else b))
        return remote(new if e == 0 else dst, dst, ps.at[e], pr.at[e], "band", other)

    for e in range(1, visits):
        spread(e, False).start()
    passed(0, False).start()
    write.start()
    for e in range(1, visits):
        spread(e, True).wait_recv()
        passed(e, False).start()
    for e in range(visits):
        passed(e, True).wait_recv()
        passed(e, False).wait_send()
    for e in range(1, visits):
        spread(e, False).wait_send()
    write.wait()
    for j, (way, d) in enumerate(order):

        @pl.when(there(way, d))
        def _():
            s = strip_of(way, d)
            for e in range(visits):
                beside(j, s, e).wait_send()
                if e:
                    across(j, s, e).wait_send()
            if d:
                hop(way, d).wait_send()


def reduce_gradient(grad, sky, strips, visits, bands):
    dma = pltpu.SemaphoreType.DMA
    hbm = pl.BlockSpec(memory_space=pl.ANY)
    piece = PW // (visits * bands)
    number = 2 * strips - 1
    block = (SROWS, piece)
    return pl.pallas_call(
        functools.partial(reduce_kernel, strips, visits, bands),
        out_shape=jax.ShapeDtypeStruct(sky.shape, f32),
        in_specs=[hbm, hbm],
        out_specs=hbm,
        scratch_shapes=[
            pltpu.VMEM((strips, visits) + block, f32),
            pltpu.VMEM((strips, visits) + block, f32),
            pltpu.VMEM((strips, visits - 1) + block, f32),
            pltpu.VMEM((2, strips) + block, f32),
            pltpu.VMEM(block, f32),
            pltpu.VMEM(block, f32),
            dma((number, visits)),
            dma,
            dma,
            dma((number, visits)),
            dma((number, visits)),
            dma((number, visits - 1)),
            dma((number, visits - 1)),
            dma((2, strips)),
            dma((2, strips)),
            dma((visits - 1,)),
            dma((visits - 1,)),
            dma((visits,)),
            dma((visits,)),
        ],
        compiler_params=pltpu.CompilerParams(
            collective_id=1, has_side_effects=True, vmem_limit_bytes=60 * 2**20
        ),
    )(grad, sky)


def on_device(observed, home_strip, column_block, psf_index, psf_coeff, weight, kernels, sky_model):
    sizes = [lax.axis_size(a) for a in ("strip", "visit", "band")]
    bank = banks(kernels)
    sky = gather_sky(sky_model, *sizes)
    grads = tile_gradients(
        home_strip, column_block, psf_index, psf_coeff, weight, sky, observed, bank
    )
    return reduce_gradient(grads, sky_model, *sizes)


def solution(mesh):
    tiles = ("groups", "strip", "visit")
    placed = (
        P(tiles, None, None),
        P(tiles, None),
        P(tiles),
        P(tiles, None),
        P(tiles, None, None),
        P(tiles),
        P(),
        P(("groups", "strip"), None),
    )
    return jax.shard_map(
        on_device,
        mesh=mesh,
        in_specs=placed,
        out_specs=P(("groups", "strip"), None),
        check_vma=False,
    )
```

```python
import functools

import jax
import jax.numpy as jnp
from jax import lax
from jax.experimental import pallas as pl
from jax.experimental.pallas import tpu as pltpu
from jax.sharding import PartitionSpec as P

PW = 4096
SROWS = 128
TW = 512
R = 8
K = 4
TPD = 16
LANE = 128
REACH = SROWS + 2 * R
MW = PW + 2 * LANE
VIEW = TW + 2 * LANE
EXT = TW + LANE
QROWS = K * LANE + LANE
f32, bf16 = jnp.float32, jnp.bfloat16
step_size = 0.5


def split(x):
    hi = x.astype(bf16)
    return hi, (x - hi.astype(f32)).astype(bf16)


def tap_sum(taps, n, side, distance):
    total = jnp.zeros(distance.shape, f32)
    for d in range(2 * R + 1):
        total = total + jnp.where(distance == d, taps[n, side * (2 * R + 1) + d], 0.0)
    return total


def build_bank(n, taps, prow, thi, tlo, colt):
    i = lax.broadcasted_iota(jnp.int32, (SROWS, 512), 0)
    j = lax.broadcasted_iota(jnp.int32, (SROWS, 512), 1)
    second, third = j >= REACH, j >= 2 * REACH
    at = j - jnp.where(second, REACH, 0) - jnp.where(third, REACH, 0)
    total = tap_sum(taps, n, 0, jnp.where(j < 3 * REACH, at - i, -1))
    hi = total.astype(bf16).astype(f32)
    prow[n] = jnp.where(second & ~third, total - hi, hi).astype(bf16)
    rows = lax.broadcasted_iota(jnp.int32, (REACH, LANE), 0)
    distance = rows - lax.broadcasted_iota(jnp.int32, (REACH, LANE), 1)
    hi, lo = split(tap_sum(taps, n, 0, distance))
    thi[n] = hi
    tlo[n] = lo
    colt[n] = tap_sum(taps, n, 1, distance)


def mm(a, b):
    return lax.dot_general(a, b, (((1,), (0,)), ((), ())), preferred_element_type=f32)


def mmt(a, b):
    return lax.dot_general(a, b, (((1,), (1,)), ((), ())), preferred_element_type=f32)


def tiles_kernel(
    meta, sky, obs, prow, thi, tlo, colt,
    acc, wcat, pcat, lhi, llo, qhi, qlo, bhi, blo, pthi, ptlo, views, seen, sems,
):
    acc[...] = jnp.zeros_like(acc)
    wcat[...] = jnp.zeros_like(wcat)
    qhi[...] = jnp.zeros_like(qhi)
    qlo[...] = jnp.zeros_like(qlo)
    band = lax.axis_index("band")
    count = TPD // lax.axis_size("band")
    lane = lax.broadcasted_iota(jnp.int32, (SROWS, LANE), 1)
    tail = lane < 2 * R
    across = (lane.astype(f32) + 0.5) / TW - 0.5

    def fetches(i):
        t, slot = band * count + i, i % 2
        top = pl.multiple_of(meta[t].astype(jnp.int32) * SROWS, SROWS)
        start = pl.multiple_of(meta[TPD + t].astype(jnp.int32) * LANE, LANE)
        return (
            pltpu.make_async_copy(
                sky.at[pl.ds(top, REACH), pl.ds(start, VIEW)], views.at[slot], sems.at[0, slot]
            ),
            pltpu.make_async_copy(obs.at[t], seen.at[slot], sems.at[1, slot]),
        )

    for copy in fetches(0):
        copy.start()

    def one(i, carry):
        t, slot = band * count + i, i % 2

        @pl.when(i + 1 < count)
        def _():
            for copy in fetches(i + 1):
                copy.start()

        for copy in fetches(i):
            copy.wait()
        top = pl.multiple_of(meta[t].astype(jnp.int32) * SROWS, SROWS)
        start = pl.multiple_of(meta[TPD + t].astype(jnp.int32) * LANE, LANE)
        window = pltpu.roll(views[slot], VIEW - (LANE - R), 1)[:, :EXT]
        whi, wlo = split(window)
        wcat[0:REACH, :] = whi
        wcat[REACH : 2 * REACH, :] = whi
        wcat[2 * REACH : 3 * REACH, :] = wlo
        for k in range(K):
            n = meta[2 * TPD + t * K + k].astype(jnp.int32)
            pcat[k * SROWS : (k + 1) * SROWS, :] = prow[n]
            pthi[:, k * SROWS : (k + 1) * SROWS] = thi[n]
            ptlo[:, k * SROWS : (k + 1) * SROWS] = tlo[n]
            taps = colt[n]
            for half in range(2):
                hi, lo = split(taps * meta[(2 + K) * TPD + t * 2 * K + 2 * k + half])
                side = slice(half * LANE, (half + 1) * LANE)
                qhi[k * LANE : (k + 1) * LANE, side] = hi[:LANE]
                qlo[k * LANE : (k + 1) * LANE, side] = lo[:LANE]
                at = K * LANE + 2 * R * k
                qhi[at : at + 2 * R, side] = hi[LANE:]
                qlo[at : at + 2 * R, side] = lo[LANE:]
        rowed = mm(pcat[...], wcat[...])
        for q in range(TW // LANE):
            rows = slice(q * LANE, (q + 1) * LANE)
            packed = jnp.zeros((SROWS, LANE), f32)
            for k in range(K):
                part = rowed[k * SROWS : (k + 1) * SROWS]
                hi, lo = split(part[:, q * LANE : (q + 1) * LANE])
                lhi[rows, k * LANE : (k + 1) * LANE] = hi
                llo[rows, k * LANE : (k + 1) * LANE] = lo
                end = jnp.where(tail, part[:, (q + 1) * LANE : (q + 2) * LANE], 0.0)
                packed = packed + (pltpu.roll(end, 2 * R * k, 1) if k else end)
            hi, lo = split(packed)
            lhi[rows, K * LANE :] = hi
            llo[rows, K * LANE :] = lo
        both = mm(lhi[...], qhi[...]) + mm(lhi[...], qlo[...]) + mm(llo[...], qhi[...])
        factor = meta[(2 + 3 * K) * TPD + t]
        spread = []
        for q in range(TW // LANE):
            rows = slice(q * LANE, (q + 1) * LANE)
            at = across + q * LANE / TW
            predicted = both[rows, :LANE] + at * both[rows, LANE:]
            weighted = factor * (predicted - seen[slot, :, q * LANE : (q + 1) * LANE])
            spread.append(jnp.concatenate([weighted, at * weighted], 1))
        shi, slo = split(jnp.concatenate(spread, 0))
        back = mmt(shi, qhi[...]) + mmt(shi, qlo[...]) + mmt(slo, qhi[...])
        for m in range(TW // LANE + 1):
            for k in range(K):
                total = 0.0
                if m < TW // LANE:
                    total = back[m * LANE : (m + 1) * LANE, k * LANE : (k + 1) * LANE]
                if m > 0:
                    end = back[(m - 1) * LANE : m * LANE, K * LANE :]
                    end = pltpu.roll(end, LANE - 2 * R * k, 1) if k else end
                    total = total + jnp.where(tail, end, 0.0)
                hi, lo = split(total)
                bhi[k * SROWS : (k + 1) * SROWS, m * LANE : (m + 1) * LANE] = hi
                blo[k * SROWS : (k + 1) * SROWS, m * LANE : (m + 1) * LANE] = lo
        grad = mm(pthi[...], bhi[...]) + mm(pthi[...], blo[...]) + mm(ptlo[...], bhi[...])
        grad = jnp.concatenate([grad, jnp.zeros((REACH, LANE), f32)], 1)
        grad = pltpu.roll(grad, LANE - R, 1)
        here = (pl.ds(top, REACH), pl.ds(start, VIEW))
        acc[here] = acc[here] + grad
        return carry

    lax.fori_loop(0, count, one, 0)


def tile_gradients(home, block, index, coeff, weight, sky, obs, bank):
    vmem = pl.BlockSpec(memory_space=pltpu.VMEM)
    smem = pl.BlockSpec(memory_space=pltpu.SMEM)
    parts = (home.astype(f32), block.astype(f32), index.astype(f32), coeff, weight)
    meta = jnp.concatenate([x.reshape(-1) for x in parts])
    return pl.pallas_call(
        tiles_kernel,
        out_shape=jax.ShapeDtypeStruct(sky.shape, f32),
        in_specs=[smem] + [pl.BlockSpec(memory_space=pl.ANY)] * 2 + [vmem] * 4,
        out_specs=vmem,
        scratch_shapes=[
            pltpu.VMEM((512, EXT), bf16),
            pltpu.VMEM((K * SROWS, 512), bf16),
            pltpu.VMEM((TW, QROWS), bf16),
            pltpu.VMEM((TW, QROWS), bf16),
            pltpu.VMEM((QROWS, 2 * LANE), bf16),
            pltpu.VMEM((QROWS, 2 * LANE), bf16),
            pltpu.VMEM((K * SROWS, EXT), bf16),
            pltpu.VMEM((K * SROWS, EXT), bf16),
            pltpu.VMEM((REACH, K * SROWS), bf16),
            pltpu.VMEM((REACH, K * SROWS), bf16),
            pltpu.VMEM((2, REACH, VIEW), f32),
            pltpu.VMEM((2, SROWS, TW), f32),
            pltpu.SemaphoreType.DMA((2, 2)),
        ],
        compiler_params=pltpu.CompilerParams(vmem_limit_bytes=56 * 2**20),
    )(meta, sky, obs, *bank)


MESH = pl.DeviceIdType.MESH
CHUNKS = 4


def greet(strips, visits, bands):
    me, v, b = (lax.axis_index(a) for a in ("strip", "visit", "band"))
    barrier = pltpu.get_barrier_semaphore()

    def signal(axis, other):
        pl.semaphore_signal(barrier, inc=1, device_id={axis: other}, device_id_type=MESH)

    @pl.when(me > 0)
    def _():
        signal("strip", me - 1)

    @pl.when(me < strips - 1)
    def _():
        signal("strip", me + 1)

    for e in range(1, visits):
        signal("visit", lax.rem(v + e, visits))
    for e in range(1, bands):
        signal("band", lax.rem(b + e, bands))

    peers = visits + bands - 2 + (me > 0).astype(jnp.int32) + (me < strips - 1).astype(jnp.int32)
    pl.semaphore_wait(barrier, peers)


def gather_kernel(
    strips, visits, bands, sky, taps, out, prow, thi, tlo, colt, edge, side,
    own_sem, edge_sem, side_sem, zs, zr, xs, xr, bs, br,
):
    me, v, b = (lax.axis_index(a) for a in ("strip", "visit", "band"))
    piece = PW // (visits * bands)
    height = SROWS // CHUNKS
    other = lax.rem(b + 1, bands)
    edge[...] = jnp.zeros_like(edge)
    side[...] = jnp.zeros_like(side)
    local = [
        pltpu.make_async_copy(
            sky,
            out.at[pl.ds(pl.multiple_of(R + me * SROWS, 8), SROWS), pl.ds(LANE, PW)],
            own_sem,
        ),
        pltpu.make_async_copy(edge, out.at[pl.ds(0, R)], edge_sem.at[0]),
        pltpu.make_async_copy(edge, out.at[pl.ds(R + strips * SROWS, R)], edge_sem.at[1]),
    ]
    for s in range(strips):
        rows = pl.ds(R + s * SROWS, SROWS)
        local.append(pltpu.make_async_copy(side, out.at[rows, pl.ds(0, LANE)], side_sem.at[0, s]))
        local.append(
            pltpu.make_async_copy(side, out.at[rows, pl.ds(LANE + PW, LANE)], side_sem.at[1, s])
        )
    greet(strips, visits, bands)

    def spot(s, c, h):
        return out.at[
            pl.ds(pl.multiple_of(R + s * SROWS + h * height, 8), height),
            pl.ds(pl.multiple_of(LANE + c * piece, LANE), piece),
        ]

    def remote(src, dst, send, recv, axis, target):
        return pltpu.make_async_remote_copy(
            src_ref=src, dst_ref=dst, send_sem=send, recv_sem=recv,
            device_id={axis: target}, device_id_type=MESH,
        )

    mine = v * bands + b

    def hop(way, d, h, incoming):
        sign = 1 if way == 0 else -1
        s = me - sign * (d if incoming else d - 1)
        dst = spot(s, mine, h)
        if d == 1 and not incoming:
            src = sky.at[
                pl.ds(h * height, height), pl.ds(pl.multiple_of(mine * piece, LANE), piece)
            ]
        else:
            src = dst
        return remote(src, dst, zs.at[way, d - 1, h], zr.at[way, d - 1, h], "strip", me + sign)

    def can_send(way, d):
        return (me < strips - 1) & (me >= d - 1) if way == 0 else (me > 0) & (me + d - 1 < strips)

    def can_get(way, d):
        return me >= d if way == 0 else me + d < strips

    def across(way, d, h, e, incoming):
        s = me - d if way == 0 else me + d
        owner = lax.rem(v - e + visits, visits) if incoming else v
        at = spot(s, owner * bands + b, h)
        return remote(
            at, at, xs.at[way, d - 1, h, e - 1], xr.at[way, d - 1, h, e - 1],
            "visit", lax.rem(v + e, visits),
        )

    def beside(way, d, h, e, incoming):
        s = me - d if way == 0 else me + d
        at = spot(s, lax.rem(v - e + visits, visits) * bands + (other if incoming else b), h)
        return remote(at, at, bs.at[way, d - 1, h, e], br.at[way, d - 1, h, e], "band", other)

    for h in range(CHUNKS):
        for way in range(2):

            @pl.when(can_send(way, 1))
            def _():
                hop(way, 1, h, False).start()

    for copy in local:
        copy.start()
    for d in range(1, strips):
        for h in range(CHUNKS):
            for way in range(2):

                @pl.when(can_get(way, d))
                def _():
                    hop(way, d, h, True).wait_recv()
                    if d + 1 < strips:

                        @pl.when(can_send(way, d + 1))
                        def _():
                            hop(way, d + 1, h, False).start()

                    for e in range(1, visits):
                        across(way, d, h, e, False).start()
                    beside(way, d, h, 0, False).start()

        if d == 1:

            def build(n, carry):
                build_bank(n, taps, prow, thi, tlo, colt)
                return carry

            lax.fori_loop(0, prow.shape[0], build, 0)

        for h in range(CHUNKS):
            for way in range(2):
                if d < 2:
                    continue

                @pl.when(can_get(way, d - 1))
                def _():
                    for e in range(1, visits):
                        across(way, d - 1, h, e, True).wait_recv()
                        beside(way, d - 1, h, e, False).start()

    for h in range(CHUNKS):
        for way in range(2):

            @pl.when(can_get(way, strips - 1))
            def _():
                for e in range(1, visits):
                    across(way, strips - 1, h, e, True).wait_recv()
                    beside(way, strips - 1, h, e, False).start()

    for d in range(1, strips):
        for h in range(CHUNKS):
            for way in range(2):

                @pl.when(can_send(way, d))
                def _():
                    hop(way, d, h, False).wait_send()

                @pl.when(can_get(way, d))
                def _():
                    for e in range(1, visits):
                        across(way, d, h, e, False).wait_send()
                    for e in range(visits):
                        beside(way, d, h, e, False).wait_send()
                        beside(way, d, h, e, True).wait_recv()

    for copy in local:
        copy.wait()


def gather_sky(sky, kernels, strips, visits, bands):
    dma = pltpu.SemaphoreType.DMA
    hbm = pl.BlockSpec(memory_space=pl.ANY)
    vmem = pl.BlockSpec(memory_space=pltpu.VMEM)
    steps, count = strips - 1, kernels.shape[0]
    return pl.pallas_call(
        functools.partial(gather_kernel, strips, visits, bands),
        out_shape=(
            jax.ShapeDtypeStruct((strips * SROWS + 2 * R, MW), f32),
            jax.ShapeDtypeStruct((count, SROWS, 512), bf16),
            jax.ShapeDtypeStruct((count, REACH, LANE), bf16),
            jax.ShapeDtypeStruct((count, REACH, LANE), bf16),
            jax.ShapeDtypeStruct((count, REACH, LANE), f32),
        ),
        in_specs=[hbm, pl.BlockSpec(memory_space=pltpu.SMEM)],
        out_specs=(hbm, vmem, vmem, vmem, vmem),
        scratch_shapes=[
            pltpu.VMEM((R, MW), f32),
            pltpu.VMEM((SROWS, LANE), f32),
            dma,
            dma((2,)),
            dma((2, strips)),
            dma((2, steps, CHUNKS)),
            dma((2, steps, CHUNKS)),
            dma((2, steps, CHUNKS, visits - 1)),
            dma((2, steps, CHUNKS, visits - 1)),
            dma((2, steps, CHUNKS, visits)),
            dma((2, steps, CHUNKS, visits)),
        ],
        compiler_params=pltpu.CompilerParams(collective_id=0, has_side_effects=True, vmem_limit_bytes=24 * 2**20),
    )(sky, kernels.reshape(count, -1))


def reduce_kernel(
    strips, visits, bands, grad, sky, out, loc, bbuf, xbuf, zbuf, mine, new,
    loc_sem, mine_sem, new_sem, bs, br, xs, xr, zs, zr, ns, nr, ps, pr,
):
    me, v, b = (lax.axis_index(a) for a in ("strip", "visit", "band"))
    piece = PW // (visits * bands)
    other = lax.rem(b + 1, bands)

    def columns(c, margin):
        return pl.ds(pl.multiple_of(margin + c * piece, LANE), piece)

    def spot(s, c):
        return grad.at[pl.ds(pl.multiple_of(R + s * SROWS, 8), SROWS), columns(c, LANE)]

    def remote(src, dst, send, recv, axis, target):
        return pltpu.make_async_remote_copy(
            src_ref=src, dst_ref=dst, send_sem=send, recv_sem=recv,
            device_id={axis: target}, device_id_type=MESH,
        )

    order = [(way, d) for d in range(strips - 1, 0, -1) for way in range(2)] + [(0, 0)]

    def strip_of(way, d):
        return me + d if way == 0 else me - d

    def there(way, d):
        return me + d < strips if way == 0 else me >= d

    def visit_at(e):
        return lax.rem(v + e, visits)

    def load(j, s, e):
        return pltpu.make_async_copy(
            spot(s, visit_at(e) * bands + b), loc.at[s, e], loc_sem.at[j, e]
        )

    def beside(j, s, e):
        return remote(
            spot(s, visit_at(e) * bands + other), bbuf.at[s, e],
            bs.at[j, e], br.at[j, e], "band", other,
        )

    def across(j, s, e):
        return remote(
            loc.at[s, e], xbuf.at[s, e - 1], xs.at[j, e - 1], xr.at[j, e - 1],
            "visit", visit_at(e),
        )

    def hop(way, d):
        sign = 1 if way == 0 else -1
        s = strip_of(way, d)
        return remote(
            loc.at[s, 0], zbuf.at[way, s], zs.at[way, d - 1], zr.at[way, d - 1],
            "strip", me + sign,
        )

    def came(way, d):
        sign = 1 if way == 0 else -1
        s = strip_of(way, d)
        return remote(
            loc.at[s, 0], zbuf.at[way, s], zs.at[way, d], zr.at[way, d], "strip", me - sign
        )

    def behind(way):
        return me > 0 if way == 0 else me < strips - 1

    keep = pltpu.make_async_copy(sky.at[:, columns(v * bands + b, 0)], mine, mine_sem)
    greet(strips, visits, bands)
    for j, (way, d) in enumerate(order):

        @pl.when(there(way, d))
        def _():
            s = strip_of(way, d)
            for e in [*range(1, visits), 0]:
                beside(j, s, e).start()
                load(j, s, e).start()

    keep.start()

    def first(j, way, d):
        s = strip_of(way, d)
        for e in [*range(1, visits), 0]:
            load(j, s, e).wait()
            beside(j, s, e).wait_recv()
            loc[s, e] = loc[s, e] + bbuf[s, e]
            if e:
                across(j, s, e).start()

    def second(j, way, d):
        s = strip_of(way, d)
        for e in range(1, visits):
            across(j, s, e).wait_recv()
            loc[s, 0] = loc[s, 0] + xbuf[s, e - 1]
        if d:

            @pl.when(behind(way))
            def _():
                came(way, d).wait_recv()
                loc[s, 0] = loc[s, 0] + zbuf[way, s]

            hop(way, d).start()

    for j, (way, d) in enumerate(order):

        @pl.when(there(way, d))
        def _():
            first(j, way, d)

    for j, (way, d) in enumerate(order):

        @pl.when(there(way, d))
        def _():
            second(j, way, d)

    for way in range(2):

        @pl.when(behind(way))
        def _():
            came(way, 0).wait_recv()
            loc[me, 0] = loc[me, 0] + zbuf[way, me]

    keep.wait()
    new[...] = jnp.maximum(mine[...] - step_size * loc[me, 0], 0.0)

    def place(c):
        return out.at[:, columns(c, 0)]

    own = v * bands + b
    write = pltpu.make_async_copy(new, place(own), new_sem)

    def spread(e, incoming):
        c = lax.rem(v - e + visits, visits) * bands + b if incoming else own
        return remote(new, place(c), ns.at[e - 1], nr.at[e - 1], "visit", visit_at(e))

    def passed(e, incoming):
        c = lax.rem(v - e + visits, visits) * bands
        dst = place(c + (other if incoming else b))
        return remote(new if e == 0 else dst, dst, ps.at[e], pr.at[e], "band", other)

    for e in range(1, visits):
        spread(e, False).start()
    passed(0, False).start()
    write.start()
    for e in range(1, visits):
        spread(e, True).wait_recv()
        passed(e, False).start()
    for e in range(visits):
        passed(e, True).wait_recv()
        passed(e, False).wait_send()
    for e in range(1, visits):
        spread(e, False).wait_send()
    write.wait()
    for j, (way, d) in enumerate(order):

        @pl.when(there(way, d))
        def _():
            s = strip_of(way, d)
            for e in range(visits):
                beside(j, s, e).wait_send()
                if e:
                    across(j, s, e).wait_send()
            if d:
                hop(way, d).wait_send()


def reduce_gradient(grad, sky, strips, visits, bands):
    dma = pltpu.SemaphoreType.DMA
    hbm = pl.BlockSpec(memory_space=pl.ANY)
    piece = PW // (visits * bands)
    number = 2 * strips - 1
    block = (SROWS, piece)
    return pl.pallas_call(
        functools.partial(reduce_kernel, strips, visits, bands),
        out_shape=jax.ShapeDtypeStruct(sky.shape, f32),
        in_specs=[hbm, hbm],
        out_specs=hbm,
        scratch_shapes=[
            pltpu.VMEM((strips, visits) + block, f32),
            pltpu.VMEM((strips, visits) + block, f32),
            pltpu.VMEM((strips, visits - 1) + block, f32),
            pltpu.VMEM((2, strips) + block, f32),
            pltpu.VMEM(block, f32),
            pltpu.VMEM(block, f32),
            dma((number, visits)),
            dma,
            dma,
            dma((number, visits)),
            dma((number, visits)),
            dma((number, visits - 1)),
            dma((number, visits - 1)),
            dma((2, strips)),
            dma((2, strips)),
            dma((visits - 1,)),
            dma((visits - 1,)),
            dma((visits,)),
            dma((visits,)),
        ],
        compiler_params=pltpu.CompilerParams(
            collective_id=1, has_side_effects=True, vmem_limit_bytes=60 * 2**20
        ),
    )(grad, sky)


def on_device(observed, home_strip, column_block, psf_index, psf_coeff, weight, kernels, sky_model):
    sizes = [lax.axis_size(a) for a in ("strip", "visit", "band")]
    sky, *bank = gather_sky(sky_model, kernels, *sizes)
    grads = tile_gradients(
        home_strip, column_block, psf_index, psf_coeff, weight, sky, observed, bank
    )
    return reduce_gradient(grads, sky_model, *sizes)


def solution(mesh):
    tiles = ("groups", "strip", "visit")
    placed = (
        P(tiles, None, None),
        P(tiles, None),
        P(tiles),
        P(tiles, None),
        P(tiles, None, None),
        P(tiles),
        P(),
        P(("groups", "strip"), None),
    )
    return jax.shard_map(
        on_device,
        mesh=mesh,
        in_specs=placed,
        out_specs=P(("groups", "strip"), None),
        check_vma=False,
    )
```
